32 devices in a mesh: groups: 2 (over x), blk: 16 (over z, y, core).
Axes of the slice: x: 2, y: 2, z: 4, core: 2. Of those that a mesh axis runs over, the one named last changes fastest.
Arguments:
- embeddings: float32 [32768, 1024], P(('groups', 'blk')), parts along dimension 0, may hold values from -16 to 16
- cluster_id: int32 [32768], P(('groups', 'blk')), parts along dimension 0, may hold values from 0 to 15, as said below
Outputs:
- nearest: float32 [32768], P(('groups', 'blk')), parts along dimension 0
The draws below stay inside these ranges and needn't reach their ends.
There are 2 independent parts, one for each index of `groups`. The reference program is written for one: setup_inputs(seed, part) draws one part's arguments, and reference() takes and returns one part's arrays. A program takes and returns all parts, laid end to end along the dimension named above; each array names one. Nothing has to cross between parts.
Inputs may be any that keep to these rules, and one draw needn't show every extreme that they name: `cluster_id`: among the rows of one index of blk no cluster appears more than 128 times, and some cluster appears exactly 128 times; every cluster has 128 or more rows in the slab.
All inputs are finite; a program needn't handle non-finite values.
Results may differ from the reference program's by a relative error of at most 0.0003.
Values may be sent and summed in bfloat16 or wider, within the bound.
A program may use at most 64 MiB of HBM per device.

```python
import math
import jax
import jax.numpy as jnp
from jax import lax

D = 1024
ROWS_DEV = 1024
SEND_CAP = 128
CLUSTERS = 16
ROWS = 16384
N_BLK = 16


def shared_clusters(key):
    key = jax.random.fold_in(key, 11)
    key_tier, key_offset, key_noise, key_shuffle = jax.random.split(key, 4)
    slots = CLUSTERS * SEND_CAP
    blocks = ROWS // ROWS_DEV
    tier = jax.random.randint(key_tier, (CLUSTERS,), 0, 4)
    offset = jax.random.randint(key_offset, (), 0, CLUSTERS)
    slot_cluster = jnp.arange(slots) // SEND_CAP
    favored = (jnp.arange(blocks) + offset) % CLUSTERS
    noise = jax.random.randint(key_noise, (blocks, slots), 0, 2 ** 14)
    score = noise + tier[slot_cluster][None, :] * 2 ** 11
    score = score + jnp.where(slot_cluster[None, :] == favored[:, None], 2 ** 17, 0)
    distinct = score * slots + jnp.arange(slots)[None, :]
    chosen_scores, chosen = lax.top_k(distinct, ROWS_DEV)
    member = chosen // SEND_CAP
    shuffle = jax.random.randint(key_shuffle, (blocks, ROWS_DEV), 0, 2 ** 20) * ROWS_DEV + jnp.arange(ROWS_DEV)[None, :]
    shuffle_scores, placing = lax.top_k(shuffle, ROWS_DEV)
    member = jnp.take_along_axis(member, placing, axis=1)
    return member.reshape(ROWS).astype(jnp.int32)


def draw_cluster_id(key, part):
    member = shared_clusters(key)
    return member


def draw_embeddings(key, part):
    member = shared_clusters(key)
    key = jax.random.fold_in(key, 5)
    key_center, key_noise, key_spread, key_pair, key_order, key_share = jax.random.split(key, 6)
    center = jax.random.normal(key_center, (CLUSTERS, D), jnp.float32)
    mixing = jax.random.permutation(key_order, ROWS).astype(jnp.int32)
    order = jnp.argsort(member * ROWS + mixing, stable=True).astype(jnp.int32)
    rank = jnp.zeros((ROWS,), jnp.int32).at[order].set(jnp.arange(ROWS, dtype=jnp.int32))
    pair_index = rank // 2
    share = jax.random.uniform(key_share, (ROWS // 2, 1), jnp.float32, 0.0, 0.95)[pair_index]
    noise = jax.random.normal(key_noise, (ROWS, D), jnp.float32)
    common = jax.random.normal(key_pair, (ROWS // 2, D), jnp.float32)[pair_index]
    spread = jnp.exp(jax.random.uniform(key_spread, (ROWS // 2, 1), jnp.float32, jnp.log(0.3), jnp.log(3.0)))[pair_index]
    mixed = jnp.sqrt(share) * common + jnp.sqrt(1.0 - share) * noise
    values = center[member] + spread * mixed
    return jnp.clip(values, -16.0, 16.0).astype(jnp.float32)


def setup_inputs(seed: int = 0, part: int = 0) -> dict:
    streams_of = jax.random.split(jax.random.key(seed), 3)
    part_splits = jax.random.split(jax.random.fold_in(streams_of[2], part), 3)
    embeddings = draw_embeddings(jax.random.fold_in(jax.random.fold_in(streams_of[2], part), 71), part)
    cluster_id = draw_cluster_id(jax.random.fold_in(jax.random.fold_in(streams_of[2], part), 71), part)
    return dict(embeddings=embeddings, cluster_id=cluster_id)


def reference(embeddings, cluster_id):
    sums = lax.optimization_barrier(jnp.sum(embeddings * embeddings, axis=1, keepdims=True))
    unit = (embeddings / jnp.sqrt(sums + 1e-06)).astype(jnp.bfloat16)
    sorted_order = jnp.argsort(cluster_id, stable=True).astype(jnp.int32)
    sorted_unit = unit[sorted_order].astype(jnp.float32)
    sorted_cluster = cluster_id[sorted_order]
    window = N_BLK * SEND_CAP
    padded_unit = jnp.pad(sorted_unit, ((window, window), (0, 0)))
    padded_cluster = jnp.pad(sorted_cluster, (window, window), constant_values=-1)
    block_rows = math.gcd(512, ROWS)
    starts = (jnp.arange(ROWS // block_rows) * block_rows).astype(jnp.int32)

    def one_block(start):
        query = lax.dynamic_slice_in_dim(padded_unit, start + window, block_rows, 0)
        query_cluster = lax.dynamic_slice_in_dim(padded_cluster, start + window, block_rows, 0)
        keys = lax.dynamic_slice_in_dim(padded_unit, start, block_rows + 2 * window, 0)
        key_cluster = lax.dynamic_slice_in_dim(padded_cluster, start, block_rows + 2 * window, 0)
        scores = jnp.dot(query, keys.T, precision=lax.Precision.HIGHEST, preferred_element_type=jnp.float32)
        query_place = start + window + jnp.arange(block_rows, dtype=jnp.int32)
        key_place = start + jnp.arange(block_rows + 2 * window, dtype=jnp.int32)
        usable = (query_cluster[:, None] == key_cluster[None, :]) & (query_place[:, None] != key_place[None, :])
        return lax.optimization_barrier(jnp.max(jnp.where(usable, scores, jnp.float32(-2.0)), axis=1))
    sorted_best = lax.map(one_block, starts).reshape(ROWS)
    return jnp.zeros((ROWS,), jnp.float32).at[sorted_order].set(sorted_best)
```

```python
import functools

import jax
import jax.numpy as jnp
from jax import lax
from jax.experimental import pallas as pl
from jax.experimental.pallas import tpu as pltpu
from jax.sharding import PartitionSpec as P

LANES = 128
CHUNK = 256
LOW = -4.0
NT = (((1,), (1,)), ((), ()))


def shift_of(place, n):
    i = n - place
    return n // 2 + (i // 2) * (2 * (i % 2) - 1)


def kernel(
    n, cap, emb_ref, id_ref, out_ref, unit, outgoing, arrived, counts_out, counts_in,
    col_bias, best_of, col_best, answers, back,
    send_sem, recv_sem, count_send, count_recv, answer_send, answer_recv,
):
    rows, width = emb_ref.shape
    slots = n * cap
    per_chunk = CHUNK // cap
    me = lax.axis_index("blk")

    barrier = pltpu.get_barrier_semaphore()

    @pl.loop(1, n)
    def _(k):
        pl.semaphore_signal(barrier, inc=1, device_id={"blk": lax.rem(me + k, n)},
                            device_id_type=pl.DeviceIdType.MESH)

    ids = id_ref[...]
    member = lax.broadcasted_iota(jnp.int32, (n, rows), 0) == ids
    one_hot = jnp.where(member, 1.0, 0.0)
    above = (
        lax.broadcasted_iota(jnp.int32, (rows, rows), 0)
        < lax.broadcasted_iota(jnp.int32, (rows, rows), 1)
    )
    earlier = jnp.dot(
        one_hot.astype(jnp.bfloat16),
        jnp.where(above, 1.0, 0.0).astype(jnp.bfloat16),
        preferred_element_type=jnp.float32,
    )
    rank = jnp.sum(earlier * one_hot, axis=0, keepdims=True).astype(jnp.int32)

    @pl.loop(0, rows // LANES)
    def _(t):
        part = pl.ds(pl.multiple_of(t * LANES, LANES), LANES)
        x = emb_ref[part, :]
        total = jnp.sum(x * x, axis=1, keepdims=True)
        unit[part, :] = (x / jnp.sqrt(total + 1e-6)).astype(jnp.bfloat16)

    def target_of(owner):
        return jnp.where(ids == owner, rank, -1)

    def block_of(target):
        pick = lax.broadcasted_iota(jnp.int32, (cap, rows), 0) == target
        pick = jnp.where(pick, 1.0, 0.0).astype(jnp.bfloat16)
        return jnp.dot(pick, unit[...], preferred_element_type=jnp.float32).astype(jnp.bfloat16)

    def count_of(target):
        count = jnp.sum(jnp.where(target >= 0, 1.0, 0.0), axis=1, keepdims=True)
        return jnp.broadcast_to(count, (8, LANES))

    remote = functools.partial(
        pltpu.make_async_remote_copy, device_id_type=pl.DeviceIdType.MESH
    )

    def owner_at(p):
        return lax.rem(me + shift_of(p, n), n)

    def rows_copy(p):
        place = pl.ds(pl.multiple_of(p * cap, cap), cap)
        return remote(outgoing.at[place], arrived.at[place], send_sem.at[p], recv_sem.at[p],
                      device_id={"blk": owner_at(p)})

    def count_copy(p):
        return remote(counts_out.at[p], counts_in.at[p], count_send.at[p], count_recv.at[p],
                      device_id={"blk": owner_at(p)})

    def answer_copy(p):
        return remote(answers.at[p], back.at[p], answer_send.at[p], answer_recv.at[p],
                      device_id={"blk": lax.rem(me - shift_of(p, n) + n, n)})

    pl.semaphore_wait(barrier, n - 1)

    @pl.loop(1, n)
    def _(i):
        p = n - i
        target = target_of(owner_at(p))
        counts_out[p] = count_of(target)
        outgoing[pl.ds(pl.multiple_of(p * cap, cap), cap), :] = block_of(target)
        count_copy(p).start()
        rows_copy(p).start()

    target = target_of(me)
    counts_in[0] = count_of(target)
    arrived[pl.ds(0, cap), :] = block_of(target)

    for j in range(slots // CHUNK):
        for p in range(j * per_chunk, (j + 1) * per_chunk):
            if p > 0:
                count_copy(p).wait_recv()
                rows_copy(p).wait_recv()
            inside = lax.broadcasted_iota(jnp.int32, (cap, LANES), 0).astype(jnp.float32)
            col_bias[pl.ds(p * cap, cap), :] = jnp.where(
                inside < counts_in[p][0:1, :], 0.0, LOW
            )
        lo = j * CHUNK
        new = arrived[pl.ds(lo, CHUNK), :]
        bias = col_bias[pl.ds(lo, CHUNK), :]
        row_bias = bias.T[0:1, :]
        own = lax.dot_general(new, new, NT, preferred_element_type=jnp.float32)
        same = (
            lax.broadcasted_iota(jnp.int32, (CHUNK, CHUNK), 0)
            == lax.broadcasted_iota(jnp.int32, (CHUNK, CHUNK), 1)
        )
        own = jnp.where(same, LOW, own + jnp.concatenate([bias] * (CHUNK // LANES), axis=1))
        col = jnp.max(own, axis=0, keepdims=True)
        if j:
            scores = lax.dot_general(
                arrived[pl.ds(0, lo), :], new, NT, preferred_element_type=jnp.float32
            )
            old_bias = col_bias[pl.ds(0, lo), :]
            keyed = scores + jnp.concatenate([old_bias] * (CHUNK // LANES), axis=1)
            col = jnp.maximum(col, jnp.max(keyed, axis=0, keepdims=True))
            masked = scores + row_bias
            best = best_of[pl.ds(0, lo), :]
            for c in range(CHUNK // LANES):
                best = jnp.maximum(best, masked[:, c * LANES:(c + 1) * LANES])
            best_of[pl.ds(0, lo), :] = best
        best_of[pl.ds(lo, CHUNK), :] = jnp.full((CHUNK, LANES), LOW, jnp.float32)
        col_best[:, pl.ds(lo, CHUNK)] = jnp.broadcast_to(col, (8, CHUNK))

    for j in range(slots // CHUNK):
        lo = j * CHUNK
        best = jnp.max(best_of[pl.ds(lo, CHUNK), :].T, axis=0, keepdims=True)
        best = jnp.maximum(best, col_best[0:1, pl.ds(lo, CHUNK)])
        for q in range(per_chunk):
            p = j * per_chunk + q
            mine = best[:, q * cap:(q + 1) * cap]
            if cap < LANES:
                mine = jnp.concatenate([mine] * (LANES // cap), axis=1)
            mine = jnp.broadcast_to(mine, (8, LANES))
            if p > 0:
                answers[p] = mine
                answer_copy(p).start()
            else:
                back[0] = mine

    @pl.loop(1, n)
    def _(p):
        answer_copy(p).wait_recv()
        rows_copy(p).wait_send()
        count_copy(p).wait_send()
        answer_copy(p).wait_send()

    table = back[:, 0, :]
    spread = jnp.where(lax.broadcasted_iota(jnp.int32, (LANES, rows), 0) == rank, 1.0, 0.0)
    picked = jnp.dot(
        table, spread, precision=lax.Precision.HIGHEST, preferred_element_type=jnp.float32
    )
    i = n - lax.broadcasted_iota(jnp.int32, (n, rows), 0)
    shift = n // 2 + jnp.where((i & 1) == 1, i >> 1, -(i >> 1))
    owner = me + jnp.where(i == n, 0, shift)
    owner = jnp.where(owner >= n, owner - n, owner)
    out_ref[...] = jnp.sum(jnp.where(owner == ids, picked, 0.0), axis=0, keepdims=True)


def body(embeddings, cluster_id):
    rows, width = embeddings.shape
    n = lax.axis_size("blk")
    cap = 2 * rows // n
    slots = n * cap
    tile = (n, 8, LANES)
    nearest = pl.pallas_call(
        functools.partial(kernel, n, cap),
        out_shape=jax.ShapeDtypeStruct((1, rows), jnp.float32),
        in_specs=[pl.BlockSpec(memory_space=pltpu.VMEM)] * 2,
        out_specs=pl.BlockSpec(memory_space=pltpu.VMEM),
        scratch_shapes=[
            pltpu.VMEM((rows, width), jnp.bfloat16),
            pltpu.VMEM((slots, width), jnp.bfloat16),
            pltpu.VMEM((slots, width), jnp.bfloat16),
            pltpu.VMEM(tile, jnp.float32),
            pltpu.VMEM(tile, jnp.float32),
            pltpu.VMEM((slots, LANES), jnp.float32),
            pltpu.VMEM((slots, LANES), jnp.float32),
            pltpu.VMEM((8, slots), jnp.float32),
            pltpu.VMEM(tile, jnp.float32),
            pltpu.VMEM(tile, jnp.float32),
        ] + [pltpu.SemaphoreType.DMA((n,))] * 6,
        compiler_params=pltpu.CompilerParams(
            collective_id=0, has_side_effects=True, vmem_limit_bytes=48 * 2**20
        ),
    )(embeddings, cluster_id.reshape(1, rows))
    return nearest.reshape(rows)


def solution(mesh):
    in_specs = (P(("groups", "blk"), None), P(("groups", "blk")))
    out_specs = P(("groups", "blk"))
    return jax.shard_map(body, mesh=mesh, in_specs=in_specs, out_specs=out_specs, check_vma=False)
```

```python
import functools
import math

import jax
import jax.numpy as jnp
from jax import lax
from jax.experimental import pallas as pl
from jax.experimental.pallas import tpu as pltpu
from jax.sharding import PartitionSpec as P

LANES = 128
GROUP = 4
LOW = -4.0
NT = (((1,), (1,)), ((), ()))


def padded_body(embeddings, cluster_id):
    local_rows, width = embeddings.shape
    owners = lax.axis_size("blk")
    capacity = 2 * local_rows // owners
    total_slots = owners * capacity
    sums = jnp.sum(embeddings * embeddings, axis=1, keepdims=True)
    unit = (embeddings / jnp.sqrt(sums + 1e-06)).astype(jnp.bfloat16)
    one_hot = (cluster_id[:, None] == jnp.arange(owners, dtype=jnp.int32)[None, :]).astype(
        jnp.int32
    )
    earlier = jnp.cumsum(one_hot, axis=0) - one_hot
    row_rank = jnp.sum(earlier * one_hot, axis=1)
    send_slot = cluster_id * capacity + row_rank
    outgoing = jnp.zeros((total_slots, width), jnp.bfloat16).at[send_slot].set(unit)
    out_flags = jnp.zeros((total_slots,), jnp.int32).at[send_slot].set(1)
    arrived, in_flags = (
        lax.all_to_all(
            outgoing.reshape(owners, capacity, width),
            "blk",
            split_axis=0,
            concat_axis=0,
            tiled=True,
        ),
        lax.all_to_all(
            out_flags.reshape(owners, capacity), "blk", split_axis=0, concat_axis=0, tiled=True
        ),
    )
    cluster_rows = arrived.reshape(total_slots, width)
    valid = in_flags.reshape(total_slots) == 1
    scores = lax.dot_general(
        cluster_rows, cluster_rows, (((1,), (1,)), ((), ())), preferred_element_type=jnp.float32
    )
    places = jnp.arange(total_slots, dtype=jnp.int32)
    usable = valid[None, :] & (places[:, None] != places[None, :])
    best_match = jnp.max(jnp.where(usable, scores, jnp.float32(-2.0)), axis=1)
    answers = lax.all_to_all(
        best_match.reshape(owners, capacity), "blk", split_axis=0, concat_axis=0, tiled=True
    )
    return answers.reshape(total_slots)[send_slot]


def kernel(
    n, parts, room, spare, chunk, emb_ref, id_ref, out_ref, over_ref, unit, outgoing, arrived,
    counts_out, counts_in, spill_out, ids_out, ids_in, col_bias, best_of, col_best, answers, back,
    flag_out, flag_in,
    send_sem, recv_sem, count_send, count_recv, answer_send, answer_recv,
    spill_send, spill_recv, ids_send, ids_recv, flag_send, flag_recv,
):
    rows, width = emb_ref.shape
    sets = n // GROUP
    total = n * (room + spare)
    me = lax.axis_index("blk")
    part = lax.axis_index("groups")
    my_set, my_place = me // GROUP, lax.rem(me, GROUP)
    remote = functools.partial(
        pltpu.make_async_remote_copy, device_id_type=pl.DeviceIdType.MESH
    )

    def owner_at(p):
        u, v = p // GROUP, p % GROUP
        return lax.rem(my_set + u, sets) * GROUP + lax.rem(my_place + v, GROUP)

    def source_at(p):
        u, v = p // GROUP, p % GROUP
        return lax.rem(my_set + sets - u, sets) * GROUP + lax.rem(my_place + GROUP - v, GROUP)

    def main_at(p):
        start = p * room + (p // (n // 2)) * (n * spare)
        return pl.ds(pl.multiple_of(start, 16), room)

    def spill_at(p):
        return pl.ds(pl.multiple_of((n // 2) * room + p * spare, 16), spare)

    def rows_copy(p):
        return remote(
            outgoing.at[pl.ds(pl.multiple_of(p * room, 16), room)], arrived.at[main_at(p)],
            send_sem.at[p], recv_sem.at[p], device_id={"blk": owner_at(p)},
        )

    def count_copy(p):
        return remote(counts_out.at[p], counts_in.at[p], count_send.at[p], count_recv.at[p],
                      device_id={"blk": owner_at(p)})

    def answer_copy(p):
        return remote(answers.at[p], back.at[p], answer_send.at[p], answer_recv.at[p],
                      device_id={"blk": source_at(p)})

    def spill_copies(u):
        p = u * GROUP
        to = {"blk": owner_at(p)}
        return (
            remote(ids_out.at[u], ids_in.at[p], ids_send.at[p], ids_recv.at[p], device_id=to),
            remote(spill_out.at[pl.ds(pl.multiple_of(u * spare, 16), spare)],
                   arrived.at[spill_at(p)], spill_send.at[p], spill_recv.at[p], device_id=to),
        )

    def relay_copies(u, v):
        first, p = u * GROUP, u * GROUP + v
        to = {"blk": my_set * GROUP + lax.rem(my_place + v, GROUP)}
        return (
            remote(ids_in.at[first], ids_in.at[p], ids_send.at[p], ids_recv.at[p], device_id=to),
            remote(arrived.at[spill_at(first)], arrived.at[spill_at(p)],
                   spill_send.at[p], spill_recv.at[p], device_id=to),
        )

    def flag_copy(x):
        return remote(flag_out, flag_in.at[x], flag_send.at[x], flag_recv.at[x],
                      device_id={"groups": lax.rem(part + x, parts), "blk": me})

    barrier = pltpu.get_barrier_semaphore()

    @pl.loop(1, n)
    def _(k):
        pl.semaphore_signal(barrier, inc=1, device_id={"blk": lax.rem(me + k, n)},
                            device_id_type=pl.DeviceIdType.MESH)

    @pl.loop(1, parts)
    def _(x):
        pl.semaphore_signal(
            barrier, inc=1, device_id={"groups": lax.rem(part + x, parts), "blk": me},
            device_id_type=pl.DeviceIdType.MESH,
        )

    ids = id_ref[...]
    index = lax.broadcasted_iota(jnp.int32, (n, rows), 0)
    above = (
        lax.broadcasted_iota(jnp.int32, (rows, rows), 0)
        < lax.broadcasted_iota(jnp.int32, (rows, rows), 1)
    )
    above = jnp.where(above, 1.0, 0.0).astype(jnp.bfloat16)

    def places(chosen):
        hot = jnp.where(chosen, 1.0, 0.0)
        earlier = jnp.dot(hot.astype(jnp.bfloat16), above, preferred_element_type=jnp.float32)
        return jnp.sum(earlier * hot, axis=0, keepdims=True).astype(jnp.int32)

    rank = places(index == ids)
    excess = rank >= room
    in_set = (ids >= index * GROUP) & (ids < index * GROUP + GROUP)
    spill_rank = places(in_set & excess)
    over = jnp.max(
        jnp.where(excess & (spill_rank >= spare), 1.0, 0.0), axis=1, keepdims=True
    )

    @pl.loop(0, rows // LANES)
    def _(t):
        some = pl.ds(pl.multiple_of(t * LANES, LANES), LANES)
        x = emb_ref[some, :]
        squares = jnp.sum(x * x, axis=1, keepdims=True)
        unit[some, :] = (x * (1.0 / jnp.sqrt(squares + 1e-6))).astype(jnp.bfloat16)

    def block_of(target, size):
        pick = lax.broadcasted_iota(jnp.int32, (size, rows), 0) == target
        pick = jnp.where(pick, 1.0, 0.0).astype(jnp.bfloat16)
        return jnp.dot(pick, unit[...], preferred_element_type=jnp.float32).astype(jnp.bfloat16)

    def target_of(owner):
        return jnp.where(ids == owner, rank, -1)

    def count_of(target):
        count = jnp.sum(jnp.where(target >= 0, 1.0, 0.0), axis=1, keepdims=True)
        first = lax.broadcasted_iota(jnp.int32, (8, LANES), 0) == 0
        return jnp.where(first, count, over)

    def spill_of(u):
        low = lax.rem(my_set + u, sets) * GROUP
        target = jnp.where((ids >= low) & (ids < low + GROUP) & excess, spill_rank, -1)
        pick = lax.broadcasted_iota(jnp.int32, (LANES, rows), 0) == target
        who = jnp.sum(jnp.where(pick, ids.astype(jnp.float32) + 1.0, 0.0), axis=1, keepdims=True)
        who = jnp.broadcast_to(who - 1.0, (LANES, LANES)).T[0:8, :]
        return who, block_of(target, spare)

    pl.semaphore_wait(barrier, n - 1 + parts - 1)

    @pl.loop(1, sets)
    def _(u):
        who, block = spill_of(u)
        ids_out[u] = who
        spill_out[pl.ds(pl.multiple_of(u * spare, 16), spare), :] = block
        for copy in spill_copies(u):
            copy.start()

    who, block = spill_of(0)
    ids_in[0] = who
    arrived[spill_at(0), :] = block

    @pl.loop(1, GROUP)
    def _(v):
        for copy in relay_copies(0, v):
            copy.start()

    @pl.loop(1, n)
    def _(p):
        target = target_of(owner_at(p))
        counts_out[p] = count_of(target)
        outgoing[pl.ds(pl.multiple_of(p * room, 16), room), :] = block_of(target, room)
        count_copy(p).start()
        rows_copy(p).start()

    target = target_of(me)
    counts_in[0] = count_of(target)
    arrived[main_at(0), :] = block_of(target, room)

    @pl.loop(1, sets)
    def _(u):
        for copy in spill_copies(u):
            copy.wait_recv()

        @pl.loop(1, GROUP)
        def _(v):
            for copy in relay_copies(u, v):
                copy.start()

    flag_out[...] = jnp.zeros((8, LANES), jnp.float32)

    def take_main(p):
        if p:
            count_copy(p).wait_recv()
            rows_copy(p).wait_recv()
        inside = lax.broadcasted_iota(jnp.int32, (room, LANES), 0).astype(jnp.float32)
        col_bias[main_at(p), :] = jnp.where(inside < counts_in[p][0:1, :], 0.0, LOW)
        flag_out[...] = jnp.maximum(flag_out[...], counts_in[p][1:2, :])

    def take_spill(p):
        if p % GROUP:
            for copy in relay_copies(p // GROUP, p % GROUP):
                copy.wait_recv()
        who = jnp.broadcast_to(ids_in[p][0:1, :], (LANES, LANES)).T[0:spare, :]
        col_bias[spill_at(p), :] = jnp.where(who == me.astype(jnp.float32), 0.0, LOW)

    order = [(take_main, p, room) for p in range(n // 2)]
    order += [(take_spill, p, spare) for p in range(n)]
    order += [(take_main, p, room) for p in range(n // 2, n)]
    end = 0
    for lo in range(0, total, chunk):
        while end < lo + chunk:
            take, p, size = order.pop(0)
            take(p)
            end += size
        new = arrived[pl.ds(lo, chunk), :]
        bias = col_bias[pl.ds(lo, chunk), :]
        row_bias = bias.T[0:1, :]
        own = lax.dot_general(new, new, NT, preferred_element_type=jnp.float32)
        same = (
            lax.broadcasted_iota(jnp.int32, (chunk, chunk), 0)
            == lax.broadcasted_iota(jnp.int32, (chunk, chunk), 1)
        )
        own = jnp.where(same, LOW, own + jnp.concatenate([bias] * (chunk // LANES), axis=1))
        col = jnp.max(own, axis=0, keepdims=True)
        if lo:
            scores = lax.dot_general(
                arrived[pl.ds(0, lo), :], new, NT, preferred_element_type=jnp.float32
            )
            old_bias = col_bias[pl.ds(0, lo), :]
            keyed = scores + jnp.concatenate([old_bias] * (chunk // LANES), axis=1)
            col = jnp.maximum(col, jnp.max(keyed, axis=0, keepdims=True))
            masked = scores + row_bias
            best = best_of[pl.ds(0, lo), :]
            for c in range(chunk // LANES):
                best = jnp.maximum(best, masked[:, c * LANES:(c + 1) * LANES])
            best_of[pl.ds(0, lo), :] = best
        best_of[pl.ds(lo, chunk), :] = jnp.full((chunk, LANES), LOW, jnp.float32)
        col_best[:, pl.ds(lo, chunk)] = jnp.broadcast_to(col, (8, chunk))

    @pl.loop(1, parts)
    def _(x):
        flag_copy(x).start()

    def best_at(lo):
        best = jnp.max(best_of[pl.ds(lo, chunk), :].T, axis=0, keepdims=True)
        return jnp.maximum(best, col_best[0:1, pl.ds(lo, chunk)])

    found = jnp.concatenate([best_at(lo) for lo in range(0, total, chunk)], axis=1)

    def lanes_of(start, size):
        filler = jnp.zeros((1, LANES - size), jnp.float32)
        return jnp.concatenate([found[:, start:start + size], filler], axis=1)

    first = lax.broadcasted_iota(jnp.int32, (8, LANES), 0) == 0
    for p in range(n):
        main = lanes_of(p * room + (p // (n // 2)) * (n * spare), room)
        spill = lanes_of((n // 2) * room + p * spare, spare)
        mine = jnp.where(first, main, spill)
        if p:
            answers[p] = mine
            answer_copy(p).start()
        else:
            back[0] = mine

    @pl.loop(1, parts)
    def _(x):
        flag_copy(x).wait_recv()
        flag_copy(x).wait_send()

    every = flag_out[...]
    for x in range(1, parts):
        every = jnp.maximum(every, flag_in[x])
    over_ref[...] = every

    @pl.loop(1, n)
    def _(p):
        answer_copy(p).wait_recv()
        rows_copy(p).wait_send()
        count_copy(p).wait_send()
        answer_copy(p).wait_send()

    @pl.loop(1, sets)
    def _(u):
        for copy in spill_copies(u):
            copy.wait_send()

    @pl.loop(0, sets)
    def _(u):
        @pl.loop(1, GROUP)
        def _(v):
            for copy in relay_copies(u, v):
                copy.wait_send()

    table = jnp.concatenate([back[:, 0, :], back[:, 1, :]], axis=1)
    where = jnp.where(excess, LANES + spill_rank, rank)
    spread = lax.broadcasted_iota(jnp.int32, (2 * LANES, rows), 0) == where
    picked = jnp.dot(
        table, jnp.where(spread, 1.0, 0.0), precision=lax.Precision.HIGHEST,
        preferred_element_type=jnp.float32,
    )
    shift = GROUP.bit_length() - 1
    owner_set = my_set + (index >> shift)
    owner_set = jnp.where(owner_set >= sets, owner_set - sets, owner_set)
    owner = owner_set * GROUP + ((my_place + (index & (GROUP - 1))) & (GROUP - 1))
    out_ref[...] = jnp.sum(jnp.where(owner == ids, picked, 0.0), axis=0, keepdims=True)


def body(embeddings, cluster_id):
    rows, width = embeddings.shape
    n = lax.axis_size("blk")
    parts = lax.axis_size("groups")
    cap = 2 * rows // n
    room = cap * 3 // 4 // 16 * 16
    spare = -(-cap * 3 // 8 // 16) * 16
    chunk = math.lcm(room, spare, LANES)
    chunk = chunk if chunk > LANES else 2 * chunk
    total = n * (room + spare)
    tile = (8, LANES)
    bf16, f32 = jnp.bfloat16, jnp.float32
    nearest, over = pl.pallas_call(
        functools.partial(kernel, n, parts, room, spare, chunk),
        out_shape=(jax.ShapeDtypeStruct((1, rows), f32), jax.ShapeDtypeStruct(tile, f32)),
        in_specs=[pl.BlockSpec(memory_space=pltpu.VMEM)] * 2,
        out_specs=[pl.BlockSpec(memory_space=pltpu.VMEM)] * 2,
        scratch_shapes=[
            pltpu.VMEM((rows, width), bf16),
            pltpu.VMEM((n * room, width), bf16),
            pltpu.VMEM((total, width), bf16),
            pltpu.VMEM((n, *tile), f32),
            pltpu.VMEM((n, *tile), f32),
            pltpu.VMEM((n // GROUP * spare, width), bf16),
            pltpu.VMEM((n // GROUP, *tile), f32),
            pltpu.VMEM((n, *tile), f32),
            pltpu.VMEM((total, LANES), f32),
            pltpu.VMEM((total, LANES), f32),
            pltpu.VMEM((8, total), f32),
            pltpu.VMEM((n, *tile), f32),
            pltpu.VMEM((n, *tile), f32),
            pltpu.VMEM(tile, f32),
            pltpu.VMEM((parts, *tile), f32),
        ] + [pltpu.SemaphoreType.DMA((n,))] * 10 + [pltpu.SemaphoreType.DMA((parts,))] * 2,
        compiler_params=pltpu.CompilerParams(
            collective_id=0, has_side_effects=True, vmem_limit_bytes=48 * 2**20
        ),
    )(embeddings, cluster_id.reshape(1, rows))
    return lax.cond(
        over[0, 0] > 0.0,
        lambda: padded_body(embeddings, cluster_id),
        lambda: nearest.reshape(rows),
    )


def solution(mesh):
    in_specs = (P(("groups", "blk"), None), P(("groups", "blk")))
    out_specs = P(("groups", "blk"))
    return jax.shard_map(body, mesh=mesh, in_specs=in_specs, out_specs=out_specs, check_vma=False)
```

```python
import functools

import jax
import jax.numpy as jnp
from jax import lax
from jax.experimental import pallas as pl
from jax.experimental.pallas import tpu as pltpu
from jax.sharding import PartitionSpec as P

LANES = 128
GROUP = 4
CHUNK = 256
LOW = -4.0
NT = (((1,), (1,)), ((), ()))


def padded_body(embeddings, cluster_id):
    local_rows, width = embeddings.shape
    owners = lax.axis_size("blk")
    capacity = 2 * local_rows // owners
    total_slots = owners * capacity
    sums = jnp.sum(embeddings * embeddings, axis=1, keepdims=True)
    unit = (embeddings / jnp.sqrt(sums + 1e-06)).astype(jnp.bfloat16)
    one_hot = (cluster_id[:, None] == jnp.arange(owners, dtype=jnp.int32)[None, :]).astype(
        jnp.int32
    )
    earlier = jnp.cumsum(one_hot, axis=0) - one_hot
    row_rank = jnp.sum(earlier * one_hot, axis=1)
    send_slot = cluster_id * capacity + row_rank
    outgoing = jnp.zeros((total_slots, width), jnp.bfloat16).at[send_slot].set(unit)
    out_flags = jnp.zeros((total_slots,), jnp.int32).at[send_slot].set(1)
    arrived, in_flags = (
        lax.all_to_all(
            outgoing.reshape(owners, capacity, width),
            "blk",
            split_axis=0,
            concat_axis=0,
            tiled=True,
        ),
        lax.all_to_all(
            out_flags.reshape(owners, capacity), "blk", split_axis=0, concat_axis=0, tiled=True
        ),
    )
    cluster_rows = arrived.reshape(total_slots, width)
    valid = in_flags.reshape(total_slots) == 1
    scores = lax.dot_general(
        cluster_rows, cluster_rows, (((1,), (1,)), ((), ())), preferred_element_type=jnp.float32
    )
    places = jnp.arange(total_slots, dtype=jnp.int32)
    usable = valid[None, :] & (places[:, None] != places[None, :])
    best_match = jnp.max(jnp.where(usable, scores, jnp.float32(-2.0)), axis=1)
    answers = lax.all_to_all(
        best_match.reshape(owners, capacity), "blk", split_axis=0, concat_axis=0, tiled=True
    )
    return answers.reshape(total_slots)[send_slot]


def kernel(
    n, parts, room, spare, chunk, emb_ref, id_ref, out_ref, over_ref, unit, outgoing, arrived,
    counts_out, counts_in, spill_out, ids_out, ids_in, col_bias, best_of, col_best, answers, back,
    flag_out, flag_in,
    send_sem, recv_sem, count_send, count_recv, answer_send, answer_recv,
    spill_send, spill_recv, ids_send, ids_recv, flag_send, flag_recv,
):
    rows, width = emb_ref.shape
    sets = n // GROUP
    total = n * (room + spare)
    me = lax.axis_index("blk")
    part = lax.axis_index("groups")
    my_set, my_place = me // GROUP, lax.rem(me, GROUP)
    remote = functools.partial(
        pltpu.make_async_remote_copy, device_id_type=pl.DeviceIdType.MESH
    )

    def owner_at(p):
        u, v = p // GROUP, p % GROUP
        return lax.rem(my_set + u, sets) * GROUP + lax.rem(my_place + v, GROUP)

    def source_at(p):
        u, v = p // GROUP, p % GROUP
        return lax.rem(my_set + sets - u, sets) * GROUP + lax.rem(my_place + GROUP - v, GROUP)

    def main_at(p):
        start = p * room + (p // (n // 2)) * (n * spare)
        return pl.ds(pl.multiple_of(start, 16), room)

    def spill_at(p):
        return pl.ds(pl.multiple_of((n // 2) * room + p * spare, 16), spare)

    def rows_copy(p):
        return remote(
            outgoing.at[pl.ds(pl.multiple_of(p * room, 16), room)], arrived.at[main_at(p)],
            send_sem.at[p], recv_sem.at[p], device_id={"blk": owner_at(p)},
        )

    def count_copy(p):
        return remote(counts_out.at[p], counts_in.at[p], count_send.at[p], count_recv.at[p],
                      device_id={"blk": owner_at(p)})

    def answer_copy(p):
        return remote(answers.at[p], back.at[p], answer_send.at[p], answer_recv.at[p],
                      device_id={"blk": source_at(p)})

    def spill_copies(u):
        p = u * GROUP
        to = {"blk": owner_at(p)}
        return (
            remote(ids_out.at[u], ids_in.at[p], ids_send.at[p], ids_recv.at[p], device_id=to),
            remote(spill_out.at[pl.ds(pl.multiple_of(u * spare, 16), spare)],
                   arrived.at[spill_at(p)], spill_send.at[p], spill_recv.at[p], device_id=to),
        )

    def relay_copies(u, v):
        first, p = u * GROUP, u * GROUP + v
        to = {"blk": my_set * GROUP + lax.rem(my_place + v, GROUP)}
        return (
            remote(ids_in.at[first], ids_in.at[p], ids_send.at[p], ids_recv.at[p], device_id=to),
            remote(arrived.at[spill_at(first)], arrived.at[spill_at(p)],
                   spill_send.at[p], spill_recv.at[p], device_id=to),
        )

    def flag_copy(x):
        return remote(flag_out, flag_in.at[x], flag_send.at[x], flag_recv.at[x],
                      device_id={"groups": lax.rem(part + x, parts), "blk": me})

    barrier = pltpu.get_barrier_semaphore()

    @pl.loop(1, n)
    def _(k):
        pl.semaphore_signal(barrier, inc=1, device_id={"blk": lax.rem(me + k, n)},
                            device_id_type=pl.DeviceIdType.MESH)

    @pl.loop(1, parts)
    def _(x):
        pl.semaphore_signal(
            barrier, inc=1, device_id={"groups": lax.rem(part + x, parts), "blk": me},
            device_id_type=pl.DeviceIdType.MESH,
        )

    ids = id_ref[...]
    index = lax.broadcasted_iota(jnp.int32, (n, rows), 0)
    above = (
        lax.broadcasted_iota(jnp.int32, (rows, rows), 0)
        < lax.broadcasted_iota(jnp.int32, (rows, rows), 1)
    )
    above = jnp.where(above, 1.0, 0.0).astype(jnp.bfloat16)

    def places(chosen):
        hot = jnp.where(chosen, 1.0, 0.0)
        earlier = jnp.dot(hot.astype(jnp.bfloat16), above, preferred_element_type=jnp.float32)
        return jnp.sum(earlier * hot, axis=0, keepdims=True).astype(jnp.int32)

    rank = places(index == ids)
    excess = rank >= room
    in_set = (ids >= index * GROUP) & (ids < index * GROUP + GROUP)
    spill_rank = places(in_set & excess)
    over = jnp.max(
        jnp.where(excess & (spill_rank >= spare), 1.0, 0.0), axis=1, keepdims=True
    )

    @pl.loop(0, rows // LANES)
    def _(t):
        some = pl.ds(pl.multiple_of(t * LANES, LANES), LANES)
        x = emb_ref[some, :]
        squares = jnp.sum(x * x, axis=1, keepdims=True)
        unit[some, :] = (x * (1.0 / jnp.sqrt(squares + 1e-6))).astype(jnp.bfloat16)

    def block_of(target, size):
        pick = lax.broadcasted_iota(jnp.int32, (size, rows), 0) == target
        pick = jnp.where(pick, 1.0, 0.0).astype(jnp.bfloat16)
        return jnp.dot(pick, unit[...], preferred_element_type=jnp.float32).astype(jnp.bfloat16)

    def target_of(owner):
        return jnp.where(ids == owner, rank, -1)

    def count_of(target):
        count = jnp.sum(jnp.where(target >= 0, 1.0, 0.0), axis=1, keepdims=True)
        first = lax.broadcasted_iota(jnp.int32, (8, LANES), 0) == 0
        return jnp.where(first, count, over)

    def spill_of(u):
        low = lax.rem(my_set + u, sets) * GROUP
        target = jnp.where((ids >= low) & (ids < low + GROUP) & excess, spill_rank, -1)
        pick = lax.broadcasted_iota(jnp.int32, (LANES, rows), 0) == target
        who = jnp.sum(jnp.where(pick, ids.astype(jnp.float32) + 1.0, 0.0), axis=1, keepdims=True)
        who = jnp.broadcast_to(who - 1.0, (LANES, LANES)).T[0:8, :]
        return who, block_of(target, spare)

    pl.semaphore_wait(barrier, n - 1 + parts - 1)

    @pl.loop(1, sets)
    def _(u):
        who, block = spill_of(u)
        ids_out[u] = who
        spill_out[pl.ds(pl.multiple_of(u * spare, 16), spare), :] = block
        for copy in spill_copies(u):
            copy.start()

    who, block = spill_of(0)
    ids_in[0] = who
    arrived[spill_at(0), :] = block

    @pl.loop(1, GROUP)
    def _(v):
        for copy in relay_copies(0, v):
            copy.start()

    @pl.loop(1, n)
    def _(p):
        target = target_of(owner_at(p))
        counts_out[p] = count_of(target)
        outgoing[pl.ds(pl.multiple_of(p * room, 16), room), :] = block_of(target, room)
        count_copy(p).start()
        rows_copy(p).start()

    target = target_of(me)
    counts_in[0] = count_of(target)
    arrived[main_at(0), :] = block_of(target, room)

    @pl.loop(1, sets)
    def _(u):
        for copy in spill_copies(u):
            copy.wait_recv()

        @pl.loop(1, GROUP)
        def _(v):
            for copy in relay_copies(u, v):
                copy.start()

    flag_out[...] = jnp.zeros((8, LANES), jnp.float32)

    def take_main(p):
        if p:
            count_copy(p).wait_recv()
            rows_copy(p).wait_recv()
        inside = lax.broadcasted_iota(jnp.int32, (room, LANES), 0).astype(jnp.float32)
        col_bias[main_at(p), :] = jnp.where(inside < counts_in[p][0:1, :], 0.0, LOW)
        flag_out[...] = jnp.maximum(flag_out[...], counts_in[p][1:2, :])

    def take_spill(p):
        if p % GROUP:
            for copy in relay_copies(p // GROUP, p % GROUP):
                copy.wait_recv()
        who = jnp.broadcast_to(ids_in[p][0:1, :], (LANES, LANES)).T[0:spare, :]
        col_bias[spill_at(p), :] = jnp.where(who == me.astype(jnp.float32), 0.0, LOW)

    order = [(take_main, p, room) for p in range(n // 2)]
    order += [(take_spill, p, spare) for p in range(n)]
    order += [(take_main, p, room) for p in range(n // 2, n)]
    end = 0
    for lo in range(0, total, chunk):
        while end < lo + chunk:
            take, p, size = order.pop(0)
            take(p)
            end += size
        new = arrived[pl.ds(lo, chunk), :]
        bias = col_bias[pl.ds(lo, chunk), :]
        row_bias = bias.T[0:1, :]
        own = lax.dot_general(new, new, NT, preferred_element_type=jnp.float32)
        same = (
            lax.broadcasted_iota(jnp.int32, (chunk, chunk), 0)
            == lax.broadcasted_iota(jnp.int32, (chunk, chunk), 1)
        )
        own = jnp.where(same, LOW, own + jnp.concatenate([bias] * (chunk // LANES), axis=1))
        col = jnp.max(own, axis=0, keepdims=True)
        if lo:
            scores = lax.dot_general(
                arrived[pl.ds(0, lo), :], new, NT, preferred_element_type=jnp.float32
            )
            old_bias = col_bias[pl.ds(0, lo), :]
            keyed = scores + jnp.concatenate([old_bias] * (chunk // LANES), axis=1)
            col = jnp.maximum(col, jnp.max(keyed, axis=0, keepdims=True))
            masked = scores + row_bias
            best = best_of[pl.ds(0, lo), :]
            for c in range(chunk // LANES):
                best = jnp.maximum(best, masked[:, c * LANES:(c + 1) * LANES])
            best_of[pl.ds(0, lo), :] = best
        best_of[pl.ds(lo, chunk), :] = jnp.full((chunk, LANES), LOW, jnp.float32)
        col_best[:, pl.ds(lo, chunk)] = jnp.broadcast_to(col, (8, chunk))

    @pl.loop(1, parts)
    def _(x):
        flag_copy(x).start()

    def best_at(lo):
        best = jnp.max(best_of[pl.ds(lo, chunk), :].T, axis=0, keepdims=True)
        return jnp.maximum(best, col_best[0:1, pl.ds(lo, chunk)])

    found = jnp.concatenate([best_at(lo) for lo in range(0, total, chunk)], axis=1)

    def lanes_of(start, size):
        filler = jnp.zeros((1, LANES - size), jnp.float32)
        return jnp.concatenate([found[:, start:start + size], filler], axis=1)

    first = lax.broadcasted_iota(jnp.int32, (8, LANES), 0) == 0
    for p in range(n):
        main = lanes_of(p * room + (p // (n // 2)) * (n * spare), room)
        spill = lanes_of((n // 2) * room + p * spare, spare)
        mine = jnp.where(first, main, spill)
        if p:
            answers[p] = mine
            answer_copy(p).start()
        else:
            back[0] = mine

    @pl.loop(1, parts)
    def _(x):
        flag_copy(x).wait_recv()
        flag_copy(x).wait_send()

    every = flag_out[...]
    for x in range(1, parts):
        every = jnp.maximum(every, flag_in[x])
    over_ref[0] = jnp.max(every)

    @pl.loop(1, n)
    def _(p):
        answer_copy(p).wait_recv()
        rows_copy(p).wait_send()
        count_copy(p).wait_send()
        answer_copy(p).wait_send()

    @pl.loop(1, sets)
    def _(u):
        for copy in spill_copies(u):
            copy.wait_send()

    @pl.loop(0, sets)
    def _(u):
        @pl.loop(1, GROUP)
        def _(v):
            for copy in relay_copies(u, v):
                copy.wait_send()

    table = jnp.concatenate([back[:, 0, :], back[:, 1, :]], axis=1)
    where = jnp.where(excess, LANES + spill_rank, rank)
    spread = lax.broadcasted_iota(jnp.int32, (2 * LANES, rows), 0) == where
    picked = jnp.dot(
        table, jnp.where(spread, 1.0, 0.0), precision=lax.Precision.HIGHEST,
        preferred_element_type=jnp.float32,
    )
    shift = GROUP.bit_length() - 1
    owner_set = my_set + (index >> shift)
    owner_set = jnp.where(owner_set >= sets, owner_set - sets, owner_set)
    owner = owner_set * GROUP + ((my_place + (index & (GROUP - 1))) & (GROUP - 1))
    out_ref[...] = jnp.sum(jnp.where(owner == ids, picked, 0.0), axis=0, keepdims=True)


def body(embeddings, cluster_id):
    rows, width = embeddings.shape
    n = lax.axis_size("blk")
    parts = lax.axis_size("groups")
    cap = 2 * rows // n
    room, spare = cap * 5 // 8 // 16 * 16, cap * 3 // 4 // 16 * 16
    total = n * (room + spare)
    tile = (8, LANES)
    bf16, f32 = jnp.bfloat16, jnp.float32
    nearest, over = pl.pallas_call(
        functools.partial(kernel, n, parts, room, spare, CHUNK),
        out_shape=(jax.ShapeDtypeStruct((1, rows), f32), jax.ShapeDtypeStruct((1,), f32)),
        in_specs=[pl.BlockSpec(memory_space=pltpu.VMEM)] * 2,
        out_specs=[pl.BlockSpec(memory_space=pltpu.VMEM), pl.BlockSpec(memory_space=pltpu.SMEM)],
        scratch_shapes=[
            pltpu.VMEM((rows, width), bf16),
            pltpu.VMEM((n * room, width), bf16),
            pltpu.VMEM((total, width), bf16),
            pltpu.VMEM((n, *tile), f32),
            pltpu.VMEM((n, *tile), f32),
            pltpu.VMEM((n // GROUP * spare, width), bf16),
            pltpu.VMEM((n // GROUP, *tile), f32),
            pltpu.VMEM((n, *tile), f32),
            pltpu.VMEM((total, LANES), f32),
            pltpu.VMEM((total, LANES), f32),
            pltpu.VMEM((8, total), f32),
            pltpu.VMEM((n, *tile), f32),
            pltpu.VMEM((n, *tile), f32),
            pltpu.VMEM(tile, f32),
            pltpu.VMEM((parts, *tile), f32),
        ] + [pltpu.SemaphoreType.DMA((n,))] * 10 + [pltpu.SemaphoreType.DMA((parts,))] * 2,
        compiler_params=pltpu.CompilerParams(
            collective_id=0, has_side_effects=True, vmem_limit_bytes=48 * 2**20
        ),
    )(embeddings, cluster_id.reshape(1, rows))
    return lax.cond(
        over[0] > 0.0,
        lambda: padded_body(embeddings, cluster_id),
        lambda: nearest.reshape(rows),
    )


def solution(mesh):
    in_specs = (P(("groups", "blk"), None), P(("groups", "blk")))
    out_specs = P(("groups", "blk"))
    return jax.shard_map(body, mesh=mesh, in_specs=in_specs, out_specs=out_specs, check_vma=False)
```
